512 devices in a mesh: ctx: 128 (over x_lo, z, y), tp: 4 (over x_hi, core).
Axes of the slice: x: 4 (x_hi: 2, x_lo: 2; x = x_hi * 2 + x_lo), y: 8, z: 8, core: 2. Of those that a mesh axis runs over, the one named last changes fastest.
Arguments:
- queries: bfloat16 [16384, 4096], P('ctx', 'tp'), may hold values from -12 to 12
- key_states: bfloat16 [16384, 1024], P('ctx', 'tp'), may hold values from -30 to 30
- value_states: bfloat16 [16384, 1024], P('ctx', 'tp'), may hold values from -6 to 6
Outputs:
- attended: bfloat16 [16384, 4096], P(('ctx', 'tp'))
The draws below stay inside these ranges and needn't reach their ends.
All inputs are finite; a program needn't handle non-finite values.
Results may differ from the reference program's by a relative error of at most 0.0049.
Values may be sent and summed in bfloat16 or wider, within the bound.
No kernel may reach another device: no remote copies, remote signals or barrier semaphores. Data moves between devices by JAX's collectives and lax.ppermute only.
A program may use at most 192 MiB of HBM per device.

```python
import math
import jax
import jax.numpy as jnp
from jax import lax

HD = 128
HQ = 32
KVH = 8
TOK_DEV = 128
HALF = 64
TOKENS = 16384
N_CTX = 128


def shared_columns(key):
    return jax.random.randint(key, (KVH, HD), 0, 2).astype(jnp.float32)


def draw_queries(key, part):
    picked = shared_columns(key)
    key = jax.random.fold_in(key, 11)
    entries = jax.random.normal(key, (TOKENS, KVH, HQ // KVH, HD), jnp.float32)
    spread = 4.0 * (1.0 - picked) + 0.2 * picked
    result = jnp.clip(entries * spread[None, :, None, :], -12.0, 12.0)
    return result.reshape(TOKENS, HQ * HD).astype(jnp.bfloat16)


def draw_key_states(key, part):
    picked = shared_columns(key)
    key = jax.random.fold_in(key, 12)
    entry_key, scale_key = jax.random.split(key)
    entries = jax.random.normal(entry_key, (TOKENS, KVH, HD), jnp.float32)
    log_scale = jax.random.uniform(scale_key, (TOKENS, KVH, 1), jnp.float32, math.log(0.3), math.log(6.0))
    spread = 1.5 * (1.0 - picked)[None, :, :] + jnp.exp(log_scale) * picked[None, :, :]
    result = jnp.clip(entries * spread, -30.0, 30.0)
    return result.reshape(TOKENS, KVH * HD).astype(jnp.bfloat16)


def shard_levels(own_key, shape, pieces, least, largest):
    def one(dim, blocks):
        steps = jax.random.uniform(jax.random.fold_in(jax.random.fold_in(own_key, 6), dim), (blocks,), jnp.float32, least / len(pieces), largest / len(pieces))
        return jnp.repeat(jnp.exp(steps), shape[dim] // blocks).reshape((-1,) + (1,) * (len(shape) - dim - 1))

    gain = one(*pieces[0])
    for cut in pieces[1:]:
        gain = gain * one(*cut)
    return gain


def scatter_about(stream_key, extent, scale, most, cuts=(), held_as=jnp.bfloat16):
    drawn = jax.random.normal(stream_key, extent, jnp.float32) * scale
    if len(cuts) > 0:
        drawn = shard_levels(stream_key, extent, cuts, -0.22, 0.18) * drawn
    return jnp.clip(drawn, min=-most, max=most).astype(held_as)


def setup_inputs(seed: int = 0) -> dict:
    arg_keys = jax.random.split(jax.random.key(seed), 4)
    queries = draw_queries(jax.random.fold_in(arg_keys[3], 71), 0)
    key_states = draw_key_states(jax.random.fold_in(arg_keys[3], 71), 0)
    value_states = scatter_about(arg_keys[2], (TOKENS, KVH * HD), 1.0, 6.0, ((0, 128), (1, 4)))
    return dict(queries=queries, key_states=key_states, value_states=value_states)


SOFT_CAP = 50.0
QUERY_SCALE = 1.0 / 12.0


def position_of(stored_rows):
    device = stored_rows // TOK_DEV
    within = stored_rows % TOK_DEV
    early = device * HALF + within
    late = (2 * N_CTX - 1 - device) * HALF + within - HALF
    return jnp.where(within < HALF, early, late).astype(jnp.int32)


def reference(queries, key_states, value_states):
    group_size = HQ // KVH
    query_all = queries.astype(jnp.float32).reshape(TOKENS, KVH, group_size, HD)
    key_all = key_states.astype(jnp.float32).reshape(TOKENS, KVH, HD)
    value_all = value_states.astype(jnp.float32).reshape(TOKENS, KVH, HD)
    key_pos = position_of(jnp.arange(TOKENS, dtype=jnp.int32))
    block_rows = 64

    def attend(block_index):
        first_row = (block_index * block_rows).astype(jnp.int32)
        query_block = lax.dynamic_slice_in_dim(query_all, first_row, block_rows, 0)
        query_pos = position_of(first_row + jnp.arange(block_rows, dtype=jnp.int32))
        scores = jnp.einsum("qkgd,rkd->kgqr", query_block, key_all, precision=lax.Precision.HIGHEST) * QUERY_SCALE
        capped = SOFT_CAP * jnp.tanh(scores / SOFT_CAP)
        allowed = key_pos[None, :] <= query_pos[:, None]
        expd = jnp.where(allowed, jnp.exp(capped), jnp.float32(0.0))
        totals = jnp.sum(expd, axis=-1)
        weights = lax.optimization_barrier(expd.astype(jnp.bfloat16)).astype(jnp.float32)
        mixed = jnp.einsum("kgqr,rkd->qkgd", weights, value_all, precision=lax.Precision.HIGHEST)
        result = mixed / jnp.transpose(totals, (2, 0, 1))[..., None]
        return result.reshape(block_rows, HQ * HD).astype(jnp.bfloat16)

    blocks = lax.map(attend, jnp.arange(TOKENS // block_rows, dtype=jnp.int32))
    return blocks.reshape(TOKENS, HQ * HD)
```

```python
import functools
import math

import jax
import jax.numpy as jnp
from jax import lax
from jax.experimental import pallas as pl
from jax.experimental.pallas import tpu as pltpu
from jax.sharding import Mesh, PartitionSpec as P

AXES = ("xl", "zh", "zm", "zl", "yh", "ym", "yl", "xh", "co")
CTX = AXES[:7]
TP = AXES[7:]
QUERY_GROUP = ("zh", "zm", "yh")
KEY_GROUP = ("xl", "zl", "ym", "yl")

HD = 128
GROUP = 4
WIDE = GROUP * HD
RANGE = 512
RANGES = 32
ARG_SCALE = 1.0 / 600.0
EXP_SCALE = 50.0 * math.log2(math.e)
STEP = 2

bf16 = jnp.bfloat16
f32 = jnp.float32


def attend_kernel(place_ref, q_ref, kv0_ref, kv1_ref, out_ref, q_scr, acc_scr, sum_scr):
    base, w_own, core, part = place_ref[0], place_ref[1], place_ref[2], place_ref[3]
    rows = GROUP * 64

    def tile_of(ref, which, t):
        late = (t >= RANGES // 2).astype(jnp.int32)
        m = jnp.where(late == 1, RANGES - 1 - t, t)
        x = (m // 8) * 2 + m % 2
        zz = (m // 2) % 4
        return ref[x, :, which, zz, :, late].reshape(128, HD)

    def tiles(which, t0):
        parts = []
        for i in range(STEP):
            parts += [tile_of(kv0_ref, which, t0 + i), tile_of(kv1_ref, which, t0 + i)]
        return jnp.concatenate(parts, axis=0)

    def chunk(k, _):
        zz, e = k % 4, k // 4
        for g in range(GROUP):
            q_scr[g * 64 : (g + 1) * 64, :] = q_ref[zz, :, e, :, g * HD : (g + 1) * HD].reshape(64, HD)
        m_early = base + 2 * zz
        m = jnp.where(e == 1, RANGES - 1 - m_early, m_early)
        acc_scr[...] = jnp.zeros_like(acc_scr)
        sum_scr[...] = jnp.zeros_like(sum_scr)

        def step(t0, masked):
            s = lax.dot_general(
                q_scr[...], tiles(0, t0), (((1,), (1,)), ((), ())), preferred_element_type=f32
            )
            w = jnp.exp2(jnp.tanh(s * ARG_SCALE) * EXP_SCALE)
            if masked:
                n = lax.broadcasted_iota(jnp.int32, w.shape, 1)
                r = lax.broadcasted_iota(jnp.int32, w.shape, 0)
                t = t0 + n // 256
                other = (n // 128) % 2
                n8 = ((n // 16) % 2) * 4 + (n // 32) % 4
                n8 = jnp.where(t >= RANGES // 2, 7 - n8, n8)
                key_core = jnp.where(other == 1, 1 - core, core)
                key_pos = t * RANGE + n8 * 64 + key_core * 32 + part * 16 + n % 16
                r8 = ((r // 32) % 2) * 4 + w_own
                r8 = jnp.where(e == 1, 7 - r8, r8)
                query_pos = m * RANGE + r8 * 64 + core * 32 + r % 32
                w = jnp.where(key_pos <= query_pos, w, 0.0)
            total = w[:, 0:HD]
            for i in range(1, w.shape[1] // HD):
                total = total + w[:, i * HD : (i + 1) * HD]
            sum_scr[...] += total
            acc_scr[...] += jnp.dot(w.astype(bf16), tiles(1, t0), preferred_element_type=f32)

        def full(i, c):
            step(i * STEP, False)
            return c

        lax.fori_loop(0, m // STEP, full, 0)
        step((m // STEP) * STEP, True)

        lane = lax.broadcasted_iota(jnp.int32, (64, HD), 1) // 16
        packed = jnp.zeros((64, HD), f32)
        for g in range(GROUP):
            piece = slice(g * 64, (g + 1) * 64)
            out_ref[zz, :, e, :, g * HD : (g + 1) * HD] = (
                acc_scr[piece, :].astype(bf16).reshape(2, 32, HD)
            )
            total = jnp.sum(sum_scr[piece, :], axis=1, keepdims=True)
            high = total.astype(bf16).astype(f32)
            packed = jnp.where(lane == 2 * g, high, packed)
            packed = jnp.where(lane == 2 * g + 1, total - high, packed)
        out_ref[zz, :, e, :, WIDE:] = packed.astype(bf16).reshape(2, 32, HD)
        return 0

    lax.fori_loop(0, 8, chunk, 0)


def attend(place, q, kv0, kv1):
    vmem = pl.BlockSpec(memory_space=pltpu.VMEM)
    return pl.pallas_call(
        attend_kernel,
        out_shape=jax.ShapeDtypeStruct(q.shape, bf16),
        in_specs=[pl.BlockSpec(memory_space=pltpu.SMEM), vmem, vmem, vmem],
        out_specs=vmem,
        scratch_shapes=[
            pltpu.VMEM((GROUP * 64, HD), bf16),
            pltpu.VMEM((GROUP * 64, HD), f32),
            pltpu.VMEM((GROUP * 64, HD), f32),
        ],
        compiler_params=pltpu.CompilerParams(vmem_limit_bytes=48 * 1024 * 1024),
        name="attend",
    )(place, q, kv0, kv1)


def finish_kernel(x_ref, out_ref):
    for xh in range(2):
        for zz in range(4):
            totals = x_ref[zz, 0, xh, :, WIDE:].astype(f32) + x_ref[zz, 1, xh, :, WIDE:].astype(f32)
            for g in range(GROUP):
                cols = slice(g * HD, (g + 1) * HD)
                mixed = x_ref[zz, 0, xh, :, cols].astype(f32) + x_ref[zz, 1, xh, :, cols].astype(f32)
                at = 32 * g
                total = totals[:, at : at + 1] + totals[:, at + 16 : at + 17]
                first = (xh * 4 + zz) * WIDE + g * HD
                out_ref[:, first : first + HD] = (mixed / total).astype(bf16)


def finish(x):
    vmem = pl.BlockSpec(memory_space=pltpu.VMEM)
    return pl.pallas_call(
        finish_kernel,
        out_shape=jax.ShapeDtypeStruct((32, 8 * WIDE), bf16),
        in_specs=[vmem],
        out_specs=vmem,
        name="finish",
    )(x)


def body(queries, keys, values):
    with jax.named_scope("to_cores"):
        mine = jnp.concatenate([queries, keys, values], axis=1).reshape(2, 2, 32, 1536)
        mine = mine.transpose(1, 0, 2, 3).reshape(2, 64, 1536)
        heads = lax.all_to_all(mine, "co", 0, 0)
    with jax.named_scope("to_heads"):
        q = heads[:, :, :1024].reshape(2, 64, 2, WIDE).transpose(0, 2, 1, 3)
        kv = heads[:, :, 1024:].reshape(2, 2, 2, 16, 2, 2, HD)
        kv = kv.transpose(0, 5, 2, 4, 1, 3, 6).reshape(2, 2, 2, 64, HD)
        q = jnp.broadcast_to(q[:, :, None], (2, 2, 2, 64, WIDE))
        sent = jnp.concatenate([q, kv], axis=-1).reshape(8, 64, WIDE + HD)
        got = lax.all_to_all(sent, QUERY_GROUP, 0, 0)
    with jax.named_scope("keys_values"):
        kv = got[:, :, WIDE:].reshape(8, 2, 2, 16, HD).transpose(1, 0, 2, 3, 4)
        spread = jnp.broadcast_to(kv[None], (16,) + kv.shape).reshape(16, -1, HD)
        kv0 = lax.all_to_all(spread, KEY_GROUP, 0, 0)
        kv1 = lax.ppermute(kv0, "co", [(0, 1), (1, 0)])
    at = {a: lax.axis_index(a) for a in AXES}
    place = jnp.stack(
        [at["xl"] * 8 + at["zl"], at["ym"] * 2 + at["yl"], at["co"], at["yh"]]
    ).astype(jnp.int32)
    shape = (4, 4, 2, 4, 2, 2, 16, HD)
    mixed = attend(place, got.reshape(4, 2, 2, 32, WIDE + HD), kv0.reshape(shape), kv1.reshape(shape))
    with jax.named_scope("to_owners"):
        owned = lax.all_to_all(mixed.reshape(16, 32, WIDE + HD), QUERY_GROUP + ("xh",), 0, 0)
    return finish(owned.reshape(4, 2, 2, 32, WIDE + HD))


def solution(mesh):
    fine = Mesh(mesh.devices.reshape((2,) * len(AXES)), AXES)
    return jax.shard_map(
        body, mesh=fine, in_specs=P(CTX, TP), out_specs=P(CTX + TP, None), check_vma=False
    )
```

```python
import functools
import math

import jax
import jax.numpy as jnp
from jax import lax
from jax.experimental import pallas as pl
from jax.experimental.pallas import tpu as pltpu
from jax.sharding import Mesh, PartitionSpec as P

AXES = ("xl", "zh", "zm", "zl", "yh", "ym", "yl", "xh", "co")
CTX = AXES[:7]
TP = AXES[7:]
QUERY_GROUP = ("xl", "zl", "yl")
KEY_GROUP = ("zh", "zm", "yh", "ym")

HD = 128
GROUP = 4
WIDE = GROUP * HD
RANGE = 512
RANGES = 32
ARG_SCALE = 1.0 / 600.0
EXP_SCALE = 50.0 * math.log2(math.e)
STEP = 8
ROWS = 512

bf16 = jnp.bfloat16
f32 = jnp.float32


def attend_kernel(place_ref, q_ref, kv0_ref, kv1_ref, out_ref, q_scr, acc_scr, sum_scr):
    base, w_own, core, part = place_ref[0], place_ref[1], place_ref[2], place_ref[3]

    def tile_of(ref, which, t):
        late = (t >= RANGES // 2).astype(jnp.int32)
        m = jnp.where(late == 1, RANGES - 1 - t, t)
        x = (m // 2) % 4
        zz = (m // 8) * 2 + m % 2
        return ref[x, :, which, zz, :, late].reshape(128, HD)

    def tiles(which, t):
        return jnp.concatenate([tile_of(kv0_ref, which, t), tile_of(kv1_ref, which, t)], axis=0)

    def key_position(t):
        n = lax.broadcasted_iota(jnp.int32, (1, 256), 1)
        n8 = (n // 16) % 8
        n8 = jnp.where(t >= RANGES // 2, 7 - n8, n8)
        key_core = jnp.where(n >= 128, 1 - core, core)
        return t * RANGE + n8 * 64 + key_core * 32 + part * 16 + n % 16

    def chunk(k, _):
        xl, e = k % 2, k // 2
        for g in range(GROUP):
            q_scr[g * 128 : (g + 1) * 128, :] = q_ref[
                pl.ds(xl * 2, 2), :, e, :, g * HD : (g + 1) * HD
            ].reshape(128, HD)
        first = base + xl * 8
        first = jnp.where(e == 1, RANGES - 2 - first, first)
        acc_scr[...] = jnp.zeros_like(acc_scr)
        sum_scr[...] = jnp.zeros_like(sum_scr)

        def scores(t):
            return lax.dot_general(
                q_scr[...], tiles(0, t), (((1,), (1,)), ((), ())), preferred_element_type=f32
            )

        def run(t0, count, masked):
            ahead = scores(t0)
            acc, total = acc_scr[...], sum_scr[...]
            for t in range(count):
                s = ahead
                if t + 1 < count:
                    ahead = scores(t0 + t + 1)
                w = jnp.exp2(jnp.tanh(s * ARG_SCALE) * EXP_SCALE)
                if masked:
                    r = lax.broadcasted_iota(jnp.int32, (ROWS, 1), 0)
                    r16 = ((r // 64) % 2) * 8 + w_own * 2 + (r // 32) % 2
                    r16 = jnp.where(e == 1, 15 - r16, r16)
                    query_pos = first * RANGE + r16 * 64 + core * 32 + r % 32
                    w = jnp.where(key_position(t0 + t) <= query_pos, w, 0.0)
                total = total + (w[:, :HD] + w[:, HD:])
                acc = acc + jnp.dot(w.astype(bf16), tiles(1, t0 + t), preferred_element_type=f32)
            acc_scr[...] = acc
            sum_scr[...] = total

        def long(i, c):
            run(i * STEP, STEP, False)
            return c

        def short(i, c):
            run(first // STEP * STEP + i * 2, 2, False)
            return c

        lax.fori_loop(0, first // STEP, long, 0)
        lax.fori_loop(0, first % STEP // 2, short, 0)
        run(first, 2, True)

        lane = lax.broadcasted_iota(jnp.int32, (128, HD), 1) // 16
        packed = jnp.zeros((128, HD), f32)
        for g in range(GROUP):
            piece = slice(g * 128, (g + 1) * 128)
            out_ref[pl.ds(xl * 2, 2), :, e, :, g * HD : (g + 1) * HD] = (
                acc_scr[piece, :].astype(bf16).reshape(2, 2, 32, HD)
            )
            total = jnp.sum(sum_scr[piece, :], axis=1, keepdims=True)
            high = total.astype(bf16).astype(f32)
            packed = jnp.where(lane == 2 * g, high, packed)
            packed = jnp.where(lane == 2 * g + 1, total - high, packed)
        out_ref[pl.ds(xl * 2, 2), :, e, :, WIDE:] = packed.astype(bf16).reshape(2, 2, 32, HD)
        return 0

    lax.fori_loop(0, 4, chunk, 0)


def attend(place, q, kv0, kv1):
    vmem = pl.BlockSpec(memory_space=pltpu.VMEM)
    return pl.pallas_call(
        attend_kernel,
        out_shape=jax.ShapeDtypeStruct(q.shape, bf16),
        in_specs=[pl.BlockSpec(memory_space=pltpu.SMEM), vmem, vmem, vmem],
        out_specs=vmem,
        scratch_shapes=[
            pltpu.VMEM((ROWS, HD), bf16),
            pltpu.VMEM((ROWS, HD), f32),
            pltpu.VMEM((ROWS, HD), f32),
        ],
        compiler_params=pltpu.CompilerParams(vmem_limit_bytes=48 * 1024 * 1024),
        name="attend",
    )(place, q, kv0, kv1)


def finish_kernel(x_ref, out_ref):
    for xh in range(2):
        for zz in range(4):
            totals = x_ref[zz, 0, xh, :, WIDE:].astype(f32) + x_ref[zz, 1, xh, :, WIDE:].astype(f32)
            for g in range(GROUP):
                cols = slice(g * HD, (g + 1) * HD)
                mixed = x_ref[zz, 0, xh, :, cols].astype(f32) + x_ref[zz, 1, xh, :, cols].astype(f32)
                at = 32 * g
                total = totals[:, at : at + 1] + totals[:, at + 16 : at + 17]
                first = (xh * 4 + zz) * WIDE + g * HD
                out_ref[:, first : first + HD] = (mixed / total).astype(bf16)


def finish(x):
    vmem = pl.BlockSpec(memory_space=pltpu.VMEM)
    return pl.pallas_call(
        finish_kernel,
        out_shape=jax.ShapeDtypeStruct((32, 8 * WIDE), bf16),
        in_specs=[vmem],
        out_specs=vmem,
        name="finish",
    )(x)


def body(queries, keys, values):
    with jax.named_scope("to_cores"):
        mine = jnp.concatenate([queries, keys, values], axis=1).reshape(2, 2, 32, 1536)
        mine = mine.transpose(1, 0, 2, 3).reshape(2, 64, 1536)
        heads = lax.all_to_all(mine, "co", 0, 0)
    with jax.named_scope("to_heads"):
        q = heads[:, :, :1024].reshape(2, 64, 2, WIDE).transpose(0, 2, 1, 3)
        kv = heads[:, :, 1024:].reshape(2, 2, 2, 16, 2, 2, HD)
        kv = kv.transpose(0, 5, 2, 4, 1, 3, 6).reshape(2, 2, 2, 64, HD)
        q = jnp.broadcast_to(q[:, :, None], (2, 2, 2, 64, WIDE))
        sent = jnp.concatenate([q, kv], axis=-1).reshape(8, 64, WIDE + HD)
        got = lax.all_to_all(sent, QUERY_GROUP, 0, 0)
    with jax.named_scope("keys_values"):
        kv = got[:, :, WIDE:].reshape(8, 2, 2, 16, HD).transpose(1, 0, 2, 3, 4)
        spread = jnp.broadcast_to(kv[None], (16,) + kv.shape).reshape(16, -1, HD)
        kv0 = lax.all_to_all(spread, KEY_GROUP, 0, 0)
        kv1 = lax.ppermute(kv0, "co", [(0, 1), (1, 0)])
    at = {a: lax.axis_index(a) for a in AXES}
    place = jnp.stack(
        [at["zh"] * 4 + at["zm"] * 2, at["yh"] * 2 + at["ym"], at["co"], at["yl"]]
    ).astype(jnp.int32)
    shape = (4, 4, 2, 4, 2, 2, 16, HD)
    mixed = attend(place, got.reshape(4, 2, 2, 32, WIDE + HD), kv0.reshape(shape), kv1.reshape(shape))
    with jax.named_scope("to_owners"):
        owned = lax.all_to_all(mixed.reshape(16, 32, WIDE + HD), QUERY_GROUP + ("xh",), 0, 0)
    return finish(owned.reshape(4, 2, 2, 32, WIDE + HD))


def solution(mesh):
    fine = Mesh(mesh.devices.reshape((2,) * len(AXES)), AXES)
    return jax.shard_map(
        body, mesh=fine, in_specs=P(CTX, TP), out_specs=P(CTX + TP, None), check_vma=False
    )
```

```python
import functools
import math

import jax
import jax.numpy as jnp
from jax import lax
from jax.experimental import pallas as pl
from jax.experimental.pallas import tpu as pltpu
from jax.sharding import Mesh, PartitionSpec as P

AXES = ("xl", "zh", "zm", "zl", "yh", "ym", "yl", "xh", "co")
CTX = AXES[:7]
TP = AXES[7:]
QUERY_GROUP = ("xl", "zl", "yl")
KEY_GROUP = ("zh", "zm", "yh", "ym")

HD = 128
GROUP = 4
WIDE = GROUP * HD
RANGE = 512
RANGES = 32
ARG_SCALE = 1.0 / 600.0
EXP_SCALE = 50.0 * math.log2(math.e)
STEP = 16
ROWS = 512

bf16 = jnp.bfloat16
f32 = jnp.float32


def attend_kernel(place_ref, q_ref, kv0_ref, kv1_ref, out_ref, q_scr, acc_scr, sum_scr):
    base, w_own, core, part = place_ref[0], place_ref[1], place_ref[2], place_ref[3]

    def tile_of(ref, which, t):
        late = (t >= RANGES // 2).astype(jnp.int32)
        m = jnp.where(late == 1, RANGES - 1 - t, t)
        x = (m // 2) % 4
        zz = (m // 8) * 2 + m % 2
        return ref[x, :, which, zz, :, late].reshape(128, HD)

    def tiles(which, t):
        return jnp.concatenate([tile_of(kv0_ref, which, t), tile_of(kv1_ref, which, t)], axis=0)

    def key_position(t):
        n = lax.broadcasted_iota(jnp.int32, (1, 256), 1)
        n8 = (n // 16) % 8
        n8 = jnp.where(t >= RANGES // 2, 7 - n8, n8)
        key_core = jnp.where(n >= 128, 1 - core, core)
        return t * RANGE + n8 * 64 + key_core * 32 + part * 16 + n % 16

    def chunk(k, _):
        xl, e = k % 2, k // 2
        for g in range(GROUP):
            q_scr[g * 128 : (g + 1) * 128, :] = q_ref[
                pl.ds(xl * 2, 2), :, e, :, g * HD : (g + 1) * HD
            ].reshape(128, HD)
        first = base + xl * 8
        first = jnp.where(e == 1, RANGES - 2 - first, first)
        acc_scr[...] = jnp.zeros_like(acc_scr)
        sum_scr[...] = jnp.zeros_like(sum_scr)

        def scores(t):
            return lax.dot_general(
                q_scr[...], tiles(0, t), (((1,), (1,)), ((), ())), preferred_element_type=f32
            )

        def run(t0, count, masked):
            ahead = scores(t0)
            acc, total = acc_scr[...], sum_scr[...]
            for t in range(count):
                s = ahead
                if t + 1 < count:
                    ahead = scores(t0 + t + 1)
                w = jnp.exp2(jnp.tanh(s * ARG_SCALE) * EXP_SCALE)
                if masked and t >= count - 2:
                    r = lax.broadcasted_iota(jnp.int32, (ROWS, 1), 0)
                    r16 = ((r // 64) % 2) * 8 + w_own * 2 + (r // 32) % 2
                    r16 = jnp.where(e == 1, 15 - r16, r16)
                    query_pos = first * RANGE + r16 * 64 + core * 32 + r % 32
                    w = jnp.where(key_position(t0 + t) <= query_pos, w, 0.0)
                total = total + (w[:, :HD] + w[:, HD:])
                acc = acc + jnp.dot(w.astype(bf16), tiles(1, t0 + t), preferred_element_type=f32)
            acc_scr[...] = acc
            sum_scr[...] = total

        def long(i, c):
            run(i * STEP, STEP, False)
            return c

        lax.fori_loop(0, first // STEP, long, 0)
        rest = first % STEP
        for count in range(0, STEP, 2):
            @pl.when(rest == count)
            def _(count=count):
                run(first - count, count + 2, True)

        lane = lax.broadcasted_iota(jnp.int32, (128, HD), 1) // 16
        packed = jnp.zeros((128, HD), f32)
        for g in range(GROUP):
            piece = slice(g * 128, (g + 1) * 128)
            out_ref[pl.ds(xl * 2, 2), :, e, :, g * HD : (g + 1) * HD] = (
                acc_scr[piece, :].astype(bf16).reshape(2, 2, 32, HD)
            )
            total = jnp.sum(sum_scr[piece, :], axis=1, keepdims=True)
            high = total.astype(bf16).astype(f32)
            packed = jnp.where(lane == 2 * g, high, packed)
            packed = jnp.where(lane == 2 * g + 1, total - high, packed)
        out_ref[pl.ds(xl * 2, 2), :, e, :, WIDE:] = packed.astype(bf16).reshape(2, 2, 32, HD)
        return 0

    lax.fori_loop(0, 4, chunk, 0)


def attend(place, q, kv0, kv1):
    vmem = pl.BlockSpec(memory_space=pltpu.VMEM)
    return pl.pallas_call(
        attend_kernel,
        out_shape=jax.ShapeDtypeStruct(q.shape, bf16),
        in_specs=[pl.BlockSpec(memory_space=pltpu.SMEM), vmem, vmem, vmem],
        out_specs=vmem,
        scratch_shapes=[
            pltpu.VMEM((ROWS, HD), bf16),
            pltpu.VMEM((ROWS, HD), f32),
            pltpu.VMEM((ROWS, HD), f32),
        ],
        compiler_params=pltpu.CompilerParams(vmem_limit_bytes=48 * 1024 * 1024),
        name="attend",
    )(place, q, kv0, kv1)


def finish_kernel(x_ref, out_ref):
    for zz in range(4):
        totals = x_ref[zz, 0, 0, :, WIDE:].astype(f32) + x_ref[zz, 1, 0, :, WIDE:].astype(f32)
        for g in range(GROUP):
            cols = slice(g * HD, (g + 1) * HD)
            mixed = x_ref[zz, 0, 0, :, cols].astype(f32) + x_ref[zz, 1, 0, :, cols].astype(f32)
            at = 32 * g
            total = totals[:, at : at + 1] + totals[:, at + 16 : at + 17]
            first = zz * WIDE + g * HD
            out_ref[:, first : first + HD] = (mixed / total).astype(bf16)


def finish(x):
    return pl.pallas_call(
        finish_kernel,
        grid=(2,),
        out_shape=jax.ShapeDtypeStruct((32, 8 * WIDE), bf16),
        in_specs=[pl.BlockSpec((4, 2, 1, 32, WIDE + HD), lambda xh: (0, 0, xh, 0, 0))],
        out_specs=pl.BlockSpec((32, 4 * WIDE), lambda xh: (0, xh)),
        name="finish",
    )(x)


def body(queries, keys, values):
    with jax.named_scope("to_cores"):
        mine = jnp.concatenate([queries, keys, values], axis=1).reshape(2, 2, 32, 1536)
        mine = mine.transpose(1, 0, 2, 3).reshape(2, 64, 1536)
        heads = lax.all_to_all(mine, "co", 0, 0)
    with jax.named_scope("to_heads"):
        q = heads[:, :, :1024].reshape(2, 64, 2, WIDE).transpose(0, 2, 1, 3)
        kv = heads[:, :, 1024:].reshape(2, 2, 2, 16, 2, 2, HD)
        kv = kv.transpose(0, 5, 2, 4, 1, 3, 6).reshape(2, 2, 2, 64, HD)
        q = jnp.broadcast_to(q[:, :, None], (2, 2, 2, 64, WIDE))
        sent = jnp.concatenate([q, kv], axis=-1).reshape(8, 64, WIDE + HD)
        got = lax.all_to_all(sent, QUERY_GROUP, 0, 0)
    with jax.named_scope("keys_values"):
        kv = got[:, :, WIDE:].reshape(8, 2, 2, 16, HD).transpose(1, 0, 2, 3, 4)
        spread = jnp.broadcast_to(kv[None], (16,) + kv.shape).reshape(16, -1, HD)
        kv0 = lax.all_to_all(spread, KEY_GROUP, 0, 0)
        kv1 = lax.ppermute(kv0, "co", [(0, 1), (1, 0)])
    at = {a: lax.axis_index(a) for a in AXES}
    place = jnp.stack(
        [at["zh"] * 4 + at["zm"] * 2, at["yh"] * 2 + at["ym"], at["co"], at["yl"]]
    ).astype(jnp.int32)
    shape = (4, 4, 2, 4, 2, 2, 16, HD)
    mixed = attend(place, got.reshape(4, 2, 2, 32, WIDE + HD), kv0.reshape(shape), kv1.reshape(shape))
    with jax.named_scope("to_owners"):
        owned = lax.all_to_all(mixed.reshape(16, 32, WIDE + HD), QUERY_GROUP + ("xh",), 0, 0)
    return finish(owned.reshape(4, 2, 2, 32, WIDE + HD))


def solution(mesh):
    fine = Mesh(mesh.devices.reshape((2,) * len(AXES)), AXES)
    return jax.shard_map(
        body, mesh=fine, in_specs=P(CTX, TP), out_specs=P(CTX + TP, None), check_vma=False
    )
```

```python
import functools
import math

import jax
import jax.numpy as jnp
from jax import lax
from jax.experimental import pallas as pl
from jax.experimental.pallas import tpu as pltpu
from jax.sharding import Mesh, PartitionSpec as P

AXES = ("xl", "zh", "zm", "zl", "yh", "ym", "yl", "xh", "co")
CTX = AXES[:7]
TP = AXES[7:]
QUERY_GROUP = ("xl", "zl", "yl")
KEY_GROUP = ("zh", "zm", "yh", "ym")

HD = 128
GROUP = 4
WIDE = GROUP * HD
RANGE = 512
RANGES = 32
ARG_SCALE = 1.0 / 600.0
EXP_SCALE = 50.0 * math.log2(math.e)
STEP = 16
ROWS = 512

bf16 = jnp.bfloat16
f32 = jnp.float32


def attend_kernel(place_ref, q_ref, kv0_ref, kv1_ref, out_ref, q_scr, acc_scr, sum_scr):
    base, w_own, core, part = place_ref[0], place_ref[1], place_ref[2], place_ref[3]

    def tile_of(ref, which, t):
        late = (t >= RANGES // 2).astype(jnp.int32)
        m = jnp.where(late == 1, RANGES - 1 - t, t)
        x = (m // 2) % 4
        zz = (m // 8) * 2 + m % 2
        return ref[x, :, which, zz, :, late].reshape(128, HD)

    def tiles(which, t):
        return jnp.concatenate([tile_of(kv0_ref, which, t), tile_of(kv1_ref, which, t)], axis=0)

    def key_position(t):
        n = lax.broadcasted_iota(jnp.int32, (1, 256), 1)
        n8 = (n // 16) % 8
        n8 = jnp.where(t >= RANGES // 2, 7 - n8, n8)
        key_core = jnp.where(n >= 128, 1 - core, core)
        return t * RANGE + n8 * 64 + key_core * 32 + part * 16 + n % 16

    def chunk(k, _):
        xl, e = k % 2, k // 2
        for g in range(GROUP):
            q_scr[g * 128 : (g + 1) * 128, :] = q_ref[
                pl.ds(xl * 2, 2), :, e, :, g * HD : (g + 1) * HD
            ].reshape(128, HD)
        first = base + xl * 8
        first = jnp.where(e == 1, RANGES - 2 - first, first)
        acc_scr[...] = jnp.zeros_like(acc_scr)
        sum_scr[...] = jnp.zeros_like(sum_scr)

        def scores(t):
            return lax.dot_general(
                q_scr[...], tiles(0, t), (((1,), (1,)), ((), ())), preferred_element_type=f32
            )

        def run(t0, count, masked):
            ahead = scores(t0)
            acc, total = acc_scr[...], sum_scr[...]
            for t in range(count):
                s = ahead
                if t + 1 < count:
                    ahead = scores(t0 + t + 1)
                w = jnp.exp2(jnp.tanh(s * ARG_SCALE) * EXP_SCALE)
                if masked and t >= count - 2:
                    r = lax.broadcasted_iota(jnp.int32, (ROWS, 1), 0)
                    r16 = ((r // 64) % 2) * 8 + w_own * 2 + (r // 32) % 2
                    r16 = jnp.where(e == 1, 15 - r16, r16)
                    query_pos = first * RANGE + r16 * 64 + core * 32 + r % 32
                    w = jnp.where(key_position(t0 + t) <= query_pos, w, 0.0)
                total = total + (w[:, :HD] + w[:, HD:])
                acc = acc + jnp.dot(w.astype(bf16), tiles(1, t0 + t), preferred_element_type=f32)
            acc_scr[...] = acc
            sum_scr[...] = total

        def long(i, c):
            run(i * STEP, STEP, False)
            return c

        lax.fori_loop(0, first // STEP, long, 0)
        rest = first % STEP
        for count in range(0, STEP, 2):
            @pl.when(rest == count)
            def _(count=count):
                run(first - count, count + 2, True)

        lane = lax.broadcasted_iota(jnp.int32, (128, HD), 1) // 16
        packed = jnp.zeros((128, HD), f32)
        for g in range(GROUP):
            piece = slice(g * 128, (g + 1) * 128)
            out_ref[pl.ds(xl * 2, 2), :, e, :, g * HD : (g + 1) * HD] = (
                acc_scr[piece, :].astype(bf16).reshape(2, 2, 32, HD)
            )
            total = jnp.sum(sum_scr[piece, :], axis=1, keepdims=True)
            high = total.astype(bf16).astype(f32)
            packed = jnp.where(lane == 2 * g, high, packed)
            packed = jnp.where(lane == 2 * g + 1, total - high, packed)
        out_ref[pl.ds(xl * 2, 2), :, e, :, WIDE:] = packed.astype(bf16).reshape(2, 2, 32, HD)
        return 0

    lax.fori_loop(0, 4, chunk, 0)


def attend(place, q, kv0, kv1):
    vmem = pl.BlockSpec(memory_space=pltpu.VMEM)
    return pl.pallas_call(
        attend_kernel,
        out_shape=jax.ShapeDtypeStruct(q.shape, bf16),
        in_specs=[pl.BlockSpec(memory_space=pltpu.SMEM), vmem, vmem, vmem],
        out_specs=vmem,
        scratch_shapes=[
            pltpu.VMEM((ROWS, HD), bf16),
            pltpu.VMEM((ROWS, HD), f32),
            pltpu.VMEM((ROWS, HD), f32),
        ],
        compiler_params=pltpu.CompilerParams(vmem_limit_bytes=48 * 1024 * 1024),
        name="attend",
    )(place, q, kv0, kv1)


def finish_kernel(x_ref, out_ref):
    for zz in range(4):
        totals = x_ref[zz, 0, 0, :, WIDE:].astype(f32) + x_ref[zz, 1, 0, :, WIDE:].astype(f32)
        for g in range(GROUP):
            cols = slice(g * HD, (g + 1) * HD)
            mixed = x_ref[zz, 0, 0, :, cols].astype(f32) + x_ref[zz, 1, 0, :, cols].astype(f32)
            at = 32 * g
            total = totals[:, at : at + 1] + totals[:, at + 16 : at + 17]
            first = zz * WIDE + g * HD
            out_ref[:, first : first + HD] = (mixed / total).astype(bf16)


def finish(x):
    return pl.pallas_call(
        finish_kernel,
        grid=(2,),
        out_shape=jax.ShapeDtypeStruct((32, 8 * WIDE), bf16),
        in_specs=[pl.BlockSpec((4, 2, 1, 32, WIDE + HD), lambda xh: (0, 0, xh, 0, 0))],
        out_specs=pl.BlockSpec((32, 4 * WIDE), lambda xh: (0, xh)),
        name="finish",
    )(x)


def body(queries, keys, values):
    with jax.named_scope("to_cores"):
        mine = jnp.concatenate([queries, keys, values], axis=1).reshape(2, 2, 32, 1536)
        mine = mine.transpose(1, 0, 2, 3).reshape(2, 64, 1536)
        core = lax.axis_index("co")
        kept = lax.dynamic_index_in_dim(mine, core, 0, keepdims=False)
        given = lax.dynamic_index_in_dim(mine, 1 - core, 0, keepdims=False)
        taken = lax.ppermute(given, "co", [(0, 1), (1, 0)])
        heads = jnp.stack([jnp.where(core == 0, kept, taken), jnp.where(core == 0, taken, kept)])
    with jax.named_scope("to_heads"):
        q = heads[:, :, :1024].reshape(2, 64, 2, WIDE).transpose(0, 2, 1, 3)
        kv = heads[:, :, 1024:].reshape(2, 2, 2, 16, 2, 2, HD)
        kv = kv.transpose(0, 5, 2, 4, 1, 3, 6).reshape(2, 2, 2, 64, HD)
        q = jnp.broadcast_to(q[:, :, None], (2, 2, 2, 64, WIDE))
        sent = jnp.concatenate([q, kv], axis=-1).reshape(8, 64, WIDE + HD)
        got = lax.all_to_all(sent, QUERY_GROUP, 0, 0)
    with jax.named_scope("keys_values"):
        kv = got[:, :, WIDE:].reshape(8, 2, 2, 16, HD).transpose(1, 0, 2, 3, 4)
        spread = jnp.broadcast_to(kv[None], (16,) + kv.shape).reshape(16, -1, HD)
        kv0 = lax.all_to_all(spread, KEY_GROUP, 0, 0)
        kv1 = lax.ppermute(kv0, "co", [(0, 1), (1, 0)])
    at = {a: lax.axis_index(a) for a in AXES}
    place = jnp.stack(
        [at["zh"] * 4 + at["zm"] * 2, at["yh"] * 2 + at["ym"], at["co"], at["yl"]]
    ).astype(jnp.int32)
    shape = (4, 4, 2, 4, 2, 2, 16, HD)
    mixed = attend(place, got.reshape(4, 2, 2, 32, WIDE + HD), kv0.reshape(shape), kv1.reshape(shape))
    with jax.named_scope("to_owners"):
        owned = lax.all_to_all(mixed.reshape(16, 32, WIDE + HD), QUERY_GROUP + ("xh",), 0, 0)
    return finish(owned.reshape(4, 2, 2, 32, WIDE + HD))


def solution(mesh):
    fine = Mesh(mesh.devices.reshape((2,) * len(AXES)), AXES)
    return jax.shard_map(
        body, mesh=fine, in_specs=P(CTX, TP), out_specs=P(CTX + TP, None), check_vma=False
    )
```

```python
import functools
import math

import jax
import jax.numpy as jnp
from jax import lax
from jax.experimental import pallas as pl
from jax.experimental.pallas import tpu as pltpu
from jax.sharding import Mesh, PartitionSpec as P

AXES = ("xl", "zh", "zm", "zl", "yh", "ym", "yl", "xh", "co")
CTX = AXES[:7]
TP = AXES[7:]
QUERY_GROUP = ("xl", "zl", "yl")
KEY_GROUP = ("zh", "zm", "yh", "ym")

HD = 128
GROUP = 4
WIDE = GROUP * HD
RANGE = 512
RANGES = 32
ARG_SCALE = 1.0 / 600.0
EXP_SCALE = 50.0 * math.log2(math.e)
STEP = 16
ROWS = 512

bf16 = jnp.bfloat16
f32 = jnp.float32


def attend_kernel(place_ref, q_ref, kv0_ref, kv1_ref, out_ref, q_scr, acc_scr, sum_scr):
    base, w_own, core, part = place_ref[0], place_ref[1], place_ref[2], place_ref[3]

    def tile_of(ref, which, t):
        late = (t >= RANGES // 2).astype(jnp.int32)
        m = jnp.where(late == 1, RANGES - 1 - t, t)
        x = (m // 2) % 4
        zz = (m // 8) * 2 + m % 2
        return ref[x, :, which, zz, :, late].reshape(128, HD)

    def tiles(which, t):
        return jnp.concatenate([tile_of(kv0_ref, which, t), tile_of(kv1_ref, which, t)], axis=0)

    def key_position(t):
        n = lax.broadcasted_iota(jnp.int32, (1, 256), 1)
        n8 = (n // 16) % 8
        n8 = jnp.where(t >= RANGES // 2, 7 - n8, n8)
        key_core = jnp.where(n >= 128, 1 - core, core)
        return t * RANGE + n8 * 64 + key_core * 32 + part * 16 + n % 16

    def chunk(k, _):
        xl, e = k % 2, k // 2
        for g in range(GROUP):
            q_scr[g * 128 : (g + 1) * 128, :] = q_ref[
                pl.ds(xl * 2, 2), :, e, :, g * HD : (g + 1) * HD
            ].reshape(128, HD)
        first = base + xl * 8
        first = jnp.where(e == 1, RANGES - 2 - first, first)
        acc_scr[...] = jnp.zeros_like(acc_scr)
        sum_scr[...] = jnp.zeros_like(sum_scr)

        def scores(t):
            return lax.dot_general(
                q_scr[...], tiles(0, t), (((1,), (1,)), ((), ())), preferred_element_type=f32
            )

        def run(t0, count, masked):
            ahead = scores(t0)
            acc, total = acc_scr[...], sum_scr[...]
            for t in range(count):
                s = ahead
                if t + 1 < count:
                    ahead = scores(t0 + t + 1)
                w = jnp.exp2(jnp.tanh(s * ARG_SCALE) * EXP_SCALE)
                if masked and t >= count - 2:
                    r = lax.broadcasted_iota(jnp.int32, (ROWS, 1), 0)
                    r16 = ((r // 64) % 2) * 8 + w_own * 2 + (r // 32) % 2
                    r16 = jnp.where(e == 1, 15 - r16, r16)
                    query_pos = first * RANGE + r16 * 64 + core * 32 + r % 32
                    w = jnp.where(key_position(t0 + t) <= query_pos, w, 0.0)
                total = total + (w[:, :HD] + w[:, HD:])
                acc = acc + jnp.dot(w.astype(bf16), tiles(1, t0 + t), preferred_element_type=f32)
            acc_scr[...] = acc
            sum_scr[...] = total

        def long(i, c):
            run(i * STEP, STEP, False)
            return c

        lax.fori_loop(0, first // STEP, long, 0)
        rest = first % STEP
        for count in range(0, STEP, 2):
            @pl.when(rest == count)
            def _(count=count):
                run(first - count, count + 2, True)

        lane = lax.broadcasted_iota(jnp.int32, (128, HD), 1) // 16
        packed = jnp.zeros((128, HD), f32)
        for g in range(GROUP):
            piece = slice(g * 128, (g + 1) * 128)
            out_ref[pl.ds(xl * 2, 2), :, e, :, g * HD : (g + 1) * HD] = (
                acc_scr[piece, :].astype(bf16).reshape(2, 2, 32, HD)
            )
            total = jnp.sum(sum_scr[piece, :], axis=1, keepdims=True)
            high = total.astype(bf16).astype(f32)
            packed = jnp.where(lane == 2 * g, high, packed)
            packed = jnp.where(lane == 2 * g + 1, total - high, packed)
        out_ref[pl.ds(xl * 2, 2), :, e, :, WIDE:] = packed.astype(bf16).reshape(2, 2, 32, HD)
        return 0

    lax.fori_loop(0, 4, chunk, 0)


def attend(place, q, kv0, kv1):
    vmem = pl.BlockSpec(memory_space=pltpu.VMEM)
    return pl.pallas_call(
        attend_kernel,
        out_shape=jax.ShapeDtypeStruct(q.shape, bf16),
        in_specs=[pl.BlockSpec(memory_space=pltpu.SMEM), vmem, vmem, vmem],
        out_specs=vmem,
        scratch_shapes=[
            pltpu.VMEM((ROWS, HD), bf16),
            pltpu.VMEM((ROWS, HD), f32),
            pltpu.VMEM((ROWS, HD), f32),
        ],
        compiler_params=pltpu.CompilerParams(vmem_limit_bytes=48 * 1024 * 1024),
        name="attend",
    )(place, q, kv0, kv1)


def finish_kernel(x_ref, out_ref):
    for zz in range(4):
        totals = x_ref[zz, 0, 0, :, WIDE:].astype(f32) + x_ref[zz, 1, 0, :, WIDE:].astype(f32)
        for g in range(GROUP):
            cols = slice(g * HD, (g + 1) * HD)
            mixed = x_ref[zz, 0, 0, :, cols].astype(f32) + x_ref[zz, 1, 0, :, cols].astype(f32)
            at = 32 * g
            total = totals[:, at : at + 1] + totals[:, at + 16 : at + 17]
            first = zz * WIDE + g * HD
            out_ref[:, first : first + HD] = (mixed / total).astype(bf16)


def finish(x):
    return pl.pallas_call(
        finish_kernel,
        grid=(2,),
        out_shape=jax.ShapeDtypeStruct((32, 8 * WIDE), bf16),
        in_specs=[pl.BlockSpec((4, 2, 1, 32, WIDE + HD), lambda xh: (0, 0, xh, 0, 0))],
        out_specs=pl.BlockSpec((32, 4 * WIDE), lambda xh: (0, xh)),
        name="finish",
    )(x)


def body(queries, keys, values):
    with jax.named_scope("to_cores"):
        core = lax.axis_index("co")

        def rows_of(one):
            parts = [x.reshape(2, 2, 32, x.shape[1]) for x in (queries, keys, values)]
            parts = [lax.dynamic_index_in_dim(x, one, 1, keepdims=False) for x in parts]
            return jnp.concatenate(parts, axis=-1).reshape(64, 1536)

        given, kept = rows_of(1 - core), rows_of(core)
        taken = lax.ppermute(given, "co", [(0, 1), (1, 0)])
        heads = jnp.stack([jnp.where(core == 0, kept, taken), jnp.where(core == 0, taken, kept)])
    with jax.named_scope("to_heads"):
        q = heads[:, :, :1024].reshape(2, 64, 2, WIDE).transpose(0, 2, 1, 3)
        kv = heads[:, :, 1024:].reshape(2, 2, 2, 16, 2, 2, HD)
        kv = kv.transpose(0, 5, 2, 4, 1, 3, 6).reshape(2, 2, 2, 64, HD)
        q = jnp.broadcast_to(q[:, :, None], (2, 2, 2, 64, WIDE))
        sent = jnp.concatenate([q, kv], axis=-1).reshape(8, 64, WIDE + HD)
        got = lax.all_to_all(sent, QUERY_GROUP, 0, 0)
    with jax.named_scope("keys_values"):
        kv = got[:, :, WIDE:].reshape(8, 2, 2, 16, HD).transpose(1, 0, 2, 3, 4)
        spread = jnp.broadcast_to(kv[None], (16,) + kv.shape).reshape(16, -1, HD)
        kv0 = lax.all_to_all(spread, KEY_GROUP, 0, 0)
        kv1 = lax.ppermute(kv0, "co", [(0, 1), (1, 0)])
    at = {a: lax.axis_index(a) for a in AXES}
    place = jnp.stack(
        [at["zh"] * 4 + at["zm"] * 2, at["yh"] * 2 + at["ym"], at["co"], at["yl"]]
    ).astype(jnp.int32)
    shape = (4, 4, 2, 4, 2, 2, 16, HD)
    mixed = attend(place, got.reshape(4, 2, 2, 32, WIDE + HD), kv0.reshape(shape), kv1.reshape(shape))
    with jax.named_scope("to_owners"):
        owned = lax.all_to_all(mixed.reshape(16, 32, WIDE + HD), QUERY_GROUP + ("xh",), 0, 0)
    return finish(owned.reshape(4, 2, 2, 32, WIDE + HD))


def solution(mesh):
    fine = Mesh(mesh.devices.reshape((2,) * len(AXES)), AXES)
    return jax.shard_map(
        body, mesh=fine, in_specs=P(CTX, TP), out_specs=P(CTX + TP, None), check_vma=False
    )
```
